512 devices in a mesh: feat: 64 (over z_hi, x, y, core), samp: 8 (over z_lo).
Axes of the slice: x: 4, y: 4, z: 16 (z_hi: 2, z_lo: 8; z = z_hi * 8 + z_lo), core: 2. Of those that a mesh axis runs over, the one named last changes fastest.
Arguments:
- samples: bfloat16 [4096, 8192], P('feat', 'samp'), may hold values from -6 to 6
- factors: bfloat16 [4096, 512], P('feat'), may hold values from -0.0546875 to 0.0546875
Outputs:
- factor_grad: float32 [4096, 512], P(('feat', 'samp'))
The draws below stay inside these ranges and needn't reach their ends.
All inputs are finite; a program needn't handle non-finite values.
Results may differ from the reference program's by a relative error of at most 0.0017.
Values may be sent and summed in bfloat16 or wider, within the bound.
A program may use at most 64 MiB of HBM per device.

```python
import math
import jax
import jax.numpy as jnp
from jax import lax

F = 4096
R = 512
SAMPLES = 8192


def draw_factors(key, part):
    key = jax.random.fold_in(key, 7)
    subkeys = jax.random.split(key, 4)
    random_part = jax.random.normal(subkeys[0], (F, R), jnp.float32)
    mixing = 0.3 * jax.random.normal(subkeys[1], (4, R), jnp.float32)
    spread = math.sqrt(10.0)
    common = jax.random.normal(subkeys[2], (F, 4), jnp.float32)
    combined = random_part
    for column in range(4):
        combined = combined + common[:, column:column + 1] * mixing[column][None, :]
    exponent = jax.random.uniform(subkeys[3], (F, 1), jnp.float32, -1.0, 1.0)
    mean_square = (spread ** 2 - spread ** (-2)) / (4.0 * math.log(spread))
    row_scale = jnp.exp(exponent * math.log(spread)) / math.sqrt(mean_square)
    values = jnp.clip(combined * row_scale, -3.5, 3.5) * F ** (-0.5)
    return values.astype(jnp.bfloat16)


def levels(stream_key, extent, pieces, smallest, top_value):
    def one(axis_at, parts):
        draws = jax.random.uniform(jax.random.fold_in(jax.random.fold_in(stream_key, 6), axis_at), (parts,), jnp.float32, smallest / len(pieces), top_value / len(pieces))
        return jnp.repeat(jnp.exp(draws), extent[axis_at] // parts).reshape((-1,) + (1,) * (len(extent) - axis_at - 1))

    level = one(*pieces[0])
    for cut in pieces[1:]:
        level = level * one(*cut)
    return level


def normal_values(stream_key, dims, scale, limit, shards=(), held_as=jnp.bfloat16):
    result = jax.random.normal(stream_key, dims, jnp.float32) * scale
    if len(shards) > 0:
        result = levels(stream_key, dims, shards, -0.22, 0.18) * result
    return jnp.clip(result, min=-limit, max=limit).astype(held_as)


def setup_inputs(seed: int = 0) -> dict:
    arg_keys = jax.random.split(jax.random.key(seed), 3)
    return {
        "samples": normal_values(arg_keys[0], (F, SAMPLES), 1.0, 6.0, ((0, 64), (1, 8))),
        "factors": draw_factors(jax.random.fold_in(arg_keys[2], 71), 0),
    }


def reference(samples, factors):
    proj = lax.dot_general(samples, factors, (((0,), (0,)), ((), ())), preferred_element_type=jnp.float32)
    squared = (proj * proj).astype(jnp.bfloat16)
    data_term = jnp.dot(samples, squared, preferred_element_type=jnp.float32)
    gram = lax.dot_general(factors, factors, (((0,), (0,)), ((), ())), preferred_element_type=jnp.float32)
    gram_sq = gram * gram
    model_term = jnp.dot(factors.astype(jnp.float32), gram_sq, precision=lax.Precision.HIGHEST)
    return 6.0 * model_term - (6.0 / SAMPLES) * data_term
```

```python
import functools

import jax
import jax.numpy as jnp
from jax import lax
from jax.experimental import pallas as pl
from jax.experimental.pallas import tpu as pltpu
from jax.sharding import PartitionSpec as P

MESH = pl.DeviceIdType.MESH
CHUNKS = ((0, 256, "x"), (256, 256, "y"), (512, 256, "x"), (768, 256, "y"), (1024, 128, "x"))
COLS = 1152
GRAM = len(CHUNKS) - 1


def contract_rows(left, right):
    return lax.dot_general(
        left, right, (((0,), (0,)), ((), ())), preferred_element_type=jnp.float32
    )


def contract_cols(left, right):
    return lax.dot_general(
        left, right, (((1,), (1,)), ((), ())), preferred_element_type=jnp.float32
    )


def kernel(sample_total, x_ref, f_ref, o_ref, xc, fc, *refs):
    n = len(CHUNKS)
    part, got1, half, got2, whole, gotz, sq = (refs[i * n:(i + 1) * n] for i in range(7))
    rows_out, rows_in, pair_send, pair_recv, send, recv, out_send, out_recv = refs[7 * n:]
    feat, samp = lax.axis_index("feat"), lax.axis_index("samp")
    core = lax.rem(feat, 2)
    at = {"y": lax.rem(lax.div(feat, 2), 4), "x": lax.rem(lax.div(feat, 8), 4)}
    stride = {"y": 2, "x": 8}

    def along(axis, step):
        there = lax.rem(at[axis] + step, 4)
        return there, (feat + (there - at[axis]) * stride[axis], samp)

    other_core = feat + 1 - 2 * core
    far = (lax.rem(feat + 32, 64), samp)
    pair = (other_core, samp)

    def row_owner(step, same):
        there = lax.rem(samp + step, 8)
        return there, (feat if same else other_core, there)

    barrier = pltpu.get_barrier_semaphore()
    partners = [along(axis, step)[1] for axis in "xy" for step in (1, 2, 3)] + [far, pair]
    partners += [row_owner(step, same)[1] for step in range(1, 8) for same in (True, False)]
    for device in partners:
        pl.semaphore_signal(barrier, inc=1, device_id=device, device_id_type=MESH)
    xc[0:64, 0:1024] = x_ref[...]
    fc[0:64, :] = f_ref[...]
    pl.semaphore_wait(barrier, len(partners))

    started = []

    def start(src, dst, send_sem, recv_sem, device):
        copy = pltpu.make_async_remote_copy(
            src_ref=src, dst_ref=dst, send_sem=send_sem, recv_sem=recv_sem,
            device_id=device, device_id_type=MESH,
        )
        copy.start()
        started.append(copy)
        return copy

    pf = start(f_ref, fc.at[64:128], pair_send.at[0], pair_recv.at[0], pair)
    px = start(x_ref, xc.at[64:128, 0:1024], pair_send.at[1], pair_recv.at[1], pair)
    pf.wait_recv()
    column = lax.broadcasted_iota(jnp.int32, (512, 128), 1)
    chosen = samp * 64 + jnp.where(column >= 64, column - 64, column)
    pick = (lax.broadcasted_iota(jnp.int32, (512, 128), 0) == chosen).astype(jnp.bfloat16)
    own_columns = jnp.dot(fc[...], pick, preferred_element_type=jnp.float32)
    xc[:, 1024:COLS] = own_columns.astype(jnp.bfloat16)
    ranks = fc[:, pl.ds(pl.multiple_of(core * 256, 256), 256)]
    px.wait_recv()

    copies = {}
    for c, (first, width, a) in enumerate(CHUNKS):
        block = contract_rows(ranks, xc[:, first:first + width])
        part[c][...] = block.reshape(4, 4, 16, width)
        for step in (1, 2, 3):
            there, device = along(a, step)
            copies[c, 0, step] = start(
                part[c].at[there], got1[c].at[step - 1],
                send.at[c, 0, step - 1], recv.at[c, 0, step - 1], device,
            )
    for c, (first, width, a) in enumerate(CHUNKS):
        b = "y" if a == "x" else "x"
        for step in (1, 2, 3):
            copies[c, 0, step].wait_recv()
        half[c][...] = (part[c][at[a]] + got1[c][0]) + (got1[c][1] + got1[c][2])
        for step in (1, 2, 3):
            there, device = along(b, step)
            copies[c, 1, step] = start(
                half[c].at[there], got2[c].at[step - 1],
                send.at[c, 1, step - 1], recv.at[c, 1, step - 1], device,
            )
    for c, (first, width, a) in enumerate(CHUNKS):
        b = "y" if a == "x" else "x"
        for step in (1, 2, 3):
            copies[c, 1, step].wait_recv()
        whole[c][...] = (half[c][at[b]] + got2[c][0]) + (got2[c][1] + got2[c][2])
        copies[c, 2] = start(whole[c], gotz[c], send.at[c, 2, 0], recv.at[c, 2, 0], far)
    for c, (first, width, a) in enumerate(CHUNKS):
        b = "y" if a == "x" else "x"
        copies[c, 2].wait_recv()
        proj = whole[c][...] + gotz[c][...]
        squared = proj * proj
        high = squared.astype(jnp.bfloat16)
        if c == GRAM:
            low = (squared - high.astype(jnp.float32)).astype(jnp.bfloat16)
            lane = lax.broadcasted_iota(jnp.int32, squared.shape, 1)
            high = jnp.where(lane >= 64, low.astype(jnp.float32), high.astype(jnp.float32))
            high = high.astype(jnp.bfloat16)
        sq[c][at[a], at[b]] = high
        for step in (1, 2, 3):
            there, device = along(b, step)
            copies[c, 3, step] = start(
                sq[c].at[at[a], at[b]], sq[c].at[at[a], at[b]],
                send.at[c, 3, step - 1], recv.at[c, 3, step - 1], device,
            )
    for c, (first, width, a) in enumerate(CHUNKS):
        for step in (1, 2, 3):
            copies[c, 3, step].wait_recv()
        for step in (1, 2, 3):
            there, device = along(a, step)
            copies[c, 4, step] = start(
                sq[c].at[at[a]], sq[c].at[at[a]],
                send.at[c, 4, step - 1], recv.at[c, 4, step - 1], device,
            )
    total = None
    for c, (first, width, a) in enumerate(CHUNKS):
        for step in (1, 2, 3):
            copies[c, 4, step].wait_recv()
        term = contract_cols(xc[:, first:first + width], sq[c][...].reshape(256, width))
        term = term * (6.0 if c == GRAM else -6.0 / sample_total)
        total = term if total is None else total + term
    rows_out[...] = total.reshape(16, 8, 256)
    done = []
    for same in (True, False):
        for step in range(8):
            slot = step + (0 if same else 8)
            there, device = row_owner(step, same)
            if slot:
                done.append(start(
                    rows_out.at[there + (0 if same else 8)], rows_in.at[slot],
                    out_send.at[slot], out_recv.at[slot], device,
                ))
    for copy in done:
        copy.wait_recv()
    own = rows_out[samp]
    for slot in range(1, 8):
        own = own + rows_in[slot]
    rest = rows_in[8]
    for slot in range(9, 16):
        rest = rest + rows_in[slot]
    o_ref[:, pl.ds(pl.multiple_of(core * 256, 256), 256)] = own
    o_ref[:, pl.ds(pl.multiple_of(256 - core * 256, 256), 256)] = rest
    for copy in started:
        copy.wait_send()


def on_device(samples, factors):
    sample_total = samples.shape[1] * lax.axis_size("samp")
    widths = [width for _, width, _ in CHUNKS]
    n = len(CHUNKS)
    scratch = [pltpu.VMEM((128, COLS), jnp.bfloat16), pltpu.VMEM((128, 512), jnp.bfloat16)]
    scratch += [pltpu.VMEM((4, 4, 16, w), jnp.float32) for w in widths]
    scratch += [pltpu.VMEM((3, 4, 16, w), jnp.float32) for w in widths]
    scratch += [pltpu.VMEM((4, 16, w), jnp.float32) for w in widths]
    scratch += [pltpu.VMEM((3, 16, w), jnp.float32) for w in widths]
    scratch += [pltpu.VMEM((16, w), jnp.float32) for w in widths]
    scratch += [pltpu.VMEM((16, w), jnp.float32) for w in widths]
    scratch += [pltpu.VMEM((4, 4, 16, w), jnp.bfloat16) for w in widths]
    scratch += [pltpu.VMEM((16, 8, 256), jnp.float32), pltpu.VMEM((16, 8, 256), jnp.float32)]
    scratch += [pltpu.SemaphoreType.DMA((2,)), pltpu.SemaphoreType.DMA((2,))]
    scratch += [pltpu.SemaphoreType.DMA((n, 5, 3)), pltpu.SemaphoreType.DMA((n, 5, 3))]
    scratch += [pltpu.SemaphoreType.DMA((16,)), pltpu.SemaphoreType.DMA((16,))]
    return pl.pallas_call(
        functools.partial(kernel, sample_total),
        out_shape=jax.ShapeDtypeStruct((8, 512), jnp.float32),
        in_specs=[pl.BlockSpec(memory_space=pltpu.VMEM)] * 2,
        out_specs=pl.BlockSpec(memory_space=pltpu.VMEM),
        scratch_shapes=scratch,
        compiler_params=pltpu.CompilerParams(
            collective_id=0, has_side_effects=True, vmem_limit_bytes=32 * 2**20
        ),
        cost_estimate=pl.CostEstimate(
            flops=2 * 128 * COLS * 256 * 2, bytes_accessed=1 << 20, transcendentals=0
        ),
    )(samples, factors)


def solution(mesh):
    in_specs = (P("feat", "samp"), P("feat", None))
    out_specs = P(("feat", "samp"), None)
    return jax.shard_map(
        on_device, mesh=mesh, in_specs=in_specs, out_specs=out_specs, check_vma=False
    )
```

```python
import functools

import jax
import jax.numpy as jnp
from jax import lax
from jax.experimental import pallas as pl
from jax.experimental.pallas import tpu as pltpu
from jax.sharding import PartitionSpec as P

MESH = pl.DeviceIdType.MESH
SIDES = (("y", "x"), ("x", "y"))
CHUNKS = ((0, 0, 256, 256), (1, 512, 256, 256), (0, 256, 256, 384), (1, 768, 256, 256))
EARLY, LATE = (0, 1), (2, 3)
GRAM = 2


def contract_rows(left, right):
    return lax.dot_general(
        left, right, (((0,), (0,)), ((), ())), preferred_element_type=jnp.float32
    )


def contract_cols(left, right):
    return lax.dot_general(
        left, right, (((1,), (1,)), ((), ())), preferred_element_type=jnp.float32
    )


def kernel(sample_total, x_ref, f_ref, o_ref, fv, *refs):
    n = len(CHUNKS)
    xs, part, gotp, half, gotr, whole, gotz, sq = (refs[n * i:n * (i + 1)] for i in range(8))
    fs, dout, din = (refs[8 * n + 2 * i:8 * n + 2 * i + 2] for i in range(3))
    rows_out, rows_in, here, local_sem, f_send, f_recv, d_send, d_recv, send, recv, out_send, out_recv = refs[8 * n + 6:]
    feat, samp = lax.axis_index("feat"), lax.axis_index("samp")
    core = lax.rem(feat, 2)
    at = {"y": lax.rem(lax.div(feat, 2), 4), "x": lax.rem(lax.div(feat, 8), 4)}
    stride = {"y": 2, "x": 8}

    def along(axis, step, device=feat):
        there = lax.rem(at[axis] + step, 4)
        return there, (device + (there - at[axis]) * stride[axis], samp)

    other_core = feat + 1 - 2 * core
    far = (lax.rem(feat + 32, 64), samp)
    pair = (other_core, samp)

    def beside(step):
        z = lax.rem(lax.div(feat, 32) * 8 + samp + step + 16, 16)
        return (lax.rem(feat, 32) + 32 * lax.div(z, 8), lax.rem(z, 8))

    def row_owner(step):
        there = lax.rem(samp + step, 8)
        return there, (feat, there)

    barrier = pltpu.get_barrier_semaphore()
    partners = [along(axis, step, device)[1] for step in (2, 1, 3) for axis in "xy" for device in (feat, other_core)]
    partners += [pair, beside(1), beside(-1)]
    for device in partners:
        pl.semaphore_signal(barrier, inc=1, device_id=device, device_id_type=MESH)
    loads = [pltpu.make_async_copy(f_ref, fv, local_sem.at[n])]
    for c, (s, first, count, width) in enumerate(CHUNKS):
        loads.append(pltpu.make_async_copy(
            x_ref.at[:, first:first + count], xs[c].at[at[SIDES[s][0]], :, 0:count], local_sem.at[c]
        ))
    for load in loads:
        load.start()
    column = lax.broadcasted_iota(jnp.int32, (512, 128), 1)
    chosen = samp * 64 + jnp.where(column >= 64, column - 64, column)
    pick = (lax.broadcasted_iota(jnp.int32, (512, 128), 0) == chosen).astype(jnp.bfloat16)
    loads[0].wait()
    own_columns = jnp.dot(fv[...], pick, preferred_element_type=jnp.float32)
    xs[GRAM][at[SIDES[0][0]], :, 256:384] = own_columns.astype(jnp.bfloat16)
    for s, (g, r) in enumerate(SIDES):
        fs[s][at[g]] = fv[:, pl.ds(pl.multiple_of(at[g] * 128, 128), 128)]
    for load in loads[1:]:
        load.wait()
    pl.semaphore_wait(barrier, len(partners))

    def tell(step):
        for device in (beside(step), beside(-step)):
            pl.semaphore_signal(here.at[step // 2], inc=1, device_id=device, device_id_type=MESH)

    def hear(step):
        pl.semaphore_wait(here.at[step // 2], 2)

    started = []

    def start(src, dst, send_sem, recv_sem, device):
        copy = pltpu.make_async_remote_copy(
            src_ref=src, dst_ref=dst, send_sem=send_sem, recv_sem=recv_sem,
            device_id=device, device_id_type=MESH,
        )
        copy.start()
        started.append(copy)
        return copy

    copies = {}
    for step in (2, 1, 3):
        for s, (g, r) in enumerate(SIDES):
            there, device = along(g, step)
            lanes = pl.ds(pl.multiple_of(there * 128, 128), 128)
            copies["f", s, step] = start(
                fv.at[:, lanes], fs[s].at[at[g]], f_send.at[s, step], f_recv.at[s, step], device
            )
    for group in (EARLY, LATE):
        if group is LATE:
            tell(1)
        for step in (2, 1, 3):
            for c in group:
                g = SIDES[CHUNKS[c][0]][0]
                there, device = along(g, step)
                copies[c, 0, step] = start(
                    xs[c].at[at[g]], xs[c].at[at[g]], send.at[c, 0, step], recv.at[c, 0, step], device
                )

    weights = []
    for s in range(2):
        for step in (1, 3, 2):
            copies["f", s, step].wait_recv()
        weights.append(jnp.transpose(fs[s][...].reshape(256, 128)))

    hear(1)
    tell(2)

    def project(c):
        s, first, count, width = CHUNKS[c]
        for step in (1, 3, 2):
            copies[c, 0, step].wait_recv()
        block = jnp.dot(weights[s], xs[c][...].reshape(256, width), preferred_element_type=jnp.float32)
        part[c][...] = block.reshape(2, 4, 16, width)
        copies[c, 1] = start(part[c].at[1 - core], gotp[c], send.at[c, 1, 0], recv.at[c, 1, 0], pair)

    def scatter(c):
        r = SIDES[CHUNKS[c][0]][1]
        copies[c, 1].wait_recv()
        half[c][...] = part[c][core] + gotp[c][...]
        for step in (2, 1, 3):
            there, device = along(r, step)
            copies[c, 2, step] = start(
                half[c].at[there], gotr[c].at[step - 1], send.at[c, 2, step], recv.at[c, 2, step], device
            )

    def exchange(c):
        r = SIDES[CHUNKS[c][0]][1]
        for step in (1, 3, 2):
            copies[c, 2, step].wait_recv()
        whole[c][...] = (half[c][at[r]] + gotr[c][0]) + (gotr[c][1] + gotr[c][2])
        copies[c, 3] = start(whole[c], gotz[c], send.at[c, 3, 0], recv.at[c, 3, 0], far)

    def square(c):
        r = SIDES[CHUNKS[c][0]][1]
        copies[c, 3].wait_recv()
        proj = whole[c][...] + gotz[c][...]
        squared = proj * proj
        high = squared.astype(jnp.bfloat16)
        own = sq[c].at[core, at[r]]
        if c == GRAM:
            own[:, 0:256] = high[:, 0:256]
            exact, wide = squared[:, 256:], high[:, 256:].astype(jnp.float32)
            lane = lax.broadcasted_iota(jnp.int32, exact.shape, 1)
            own[:, 256:] = jnp.where(lane >= 64, exact - wide, wide).astype(jnp.bfloat16)
        else:
            own[...] = high
        for step in (2, 1, 3):
            for stage, core_there in ((4, feat), (5, other_core)):
                there, device = along(r, step, core_there)
                copies[c, stage, step] = start(own, own, send.at[c, stage, step], recv.at[c, stage, step], device)
        copies[c, 5, 0] = start(own, own, send.at[c, 5, 0], recv.at[c, 5, 0], pair)

    def term(c):
        s, first, count, width = CHUNKS[c]
        copies[c, 5, 0].wait_recv()
        for step in (1, 3, 2):
            copies[c, 4, step].wait_recv()
            copies[c, 5, step].wait_recv()
        left, right = xs[c][...].reshape(256, width), sq[c][...].reshape(128, width)
        product = (-6.0 / sample_total) * contract_cols(left[:, 0:count], right[:, 0:count])
        if c == GRAM:
            product = product + 6.0 * contract_cols(left[:, count:], right[:, count:])
        return product

    for c in EARLY:
        project(c)
    hear(2)
    tell(4)
    for c in EARLY:
        scatter(c)
    for c in LATE:
        project(c)
    for c in LATE:
        scatter(c)
    hear(4)
    for c in EARLY + LATE:
        exchange(c)
    for c in EARLY + LATE:
        square(c)
    total = [0.0, 0.0]
    for group in (EARLY, LATE):
        for c in group:
            s = CHUNKS[c][0]
            total[s] = total[s] + term(c)
            if c in LATE:
                g = SIDES[s][0]
                dout[s][...] = total[s].reshape(4, 64, 128)
                for step in (2, 1, 3):
                    there, device = along(g, step)
                    copies["d", s, step] = start(
                        dout[s].at[there], din[s].at[at[g]], d_send.at[s, step], d_recv.at[s, step], device
                    )
                din[s][at[g]] = dout[s][at[g]]
    for step in (1, 3, 2):
        for s in range(2):
            copies["d", s, step].wait_recv()
    for chunk in range(4):
        rows_out[:, chunk] = (din[0][chunk] + din[1][chunk]).reshape(8, 8, 128)
    done = []
    for step in (4, 3, 5, 2, 6, 1, 7):
        there, device = row_owner(step)
        done.append(start(
            rows_out.at[there], rows_in.at[step - 1],
            out_send.at[step - 1], out_recv.at[step - 1], device,
        ))
    for copy in started[:-7]:
        copy.wait_send()
    for copy in done:
        copy.wait_recv()
    own = rows_out[samp]
    for slot in range(7):
        own = own + rows_in[slot]
    for chunk in range(4):
        o_ref[:, chunk * 128:(chunk + 1) * 128] = own[chunk]
    for copy in done:
        copy.wait_send()


def on_device(samples, factors):
    sample_total = samples.shape[1] * lax.axis_size("samp")
    n = len(CHUNKS)

    def each(shape, dtype):
        return [pltpu.VMEM(shape + (width,), dtype) for _, _, _, width in CHUNKS]

    scratch = [pltpu.VMEM((64, 512), jnp.bfloat16)]
    scratch += each((4, 64), jnp.bfloat16)
    scratch += each((2, 4, 16), jnp.float32)
    scratch += each((4, 16), jnp.float32)
    scratch += each((4, 16), jnp.float32)
    scratch += each((3, 16), jnp.float32)
    scratch += each((16,), jnp.float32)
    scratch += each((16,), jnp.float32)
    scratch += each((2, 4, 16), jnp.bfloat16)
    scratch += [pltpu.VMEM((4, 64, 128), jnp.bfloat16)] * 2
    scratch += [pltpu.VMEM((4, 64, 128), jnp.float32)] * 4
    scratch += [pltpu.VMEM((8, 4, 8, 128), jnp.float32), pltpu.VMEM((7, 4, 8, 128), jnp.float32)]
    scratch += [pltpu.SemaphoreType.REGULAR((3,)), pltpu.SemaphoreType.DMA((n + 1,))]
    scratch += [pltpu.SemaphoreType.DMA((2, 4))] * 4
    scratch += [pltpu.SemaphoreType.DMA((n, 6, 4)), pltpu.SemaphoreType.DMA((n, 6, 4))]
    scratch += [pltpu.SemaphoreType.DMA((7,)), pltpu.SemaphoreType.DMA((7,))]
    return pl.pallas_call(
        functools.partial(kernel, sample_total),
        out_shape=pltpu.VMEM((8, 512), jnp.float32),
        in_specs=[pl.BlockSpec(memory_space=pltpu.HBM)] * 2,
        out_specs=pl.BlockSpec(memory_space=pltpu.VMEM),
        scratch_shapes=scratch,
        compiler_params=pltpu.CompilerParams(
            collective_id=0, has_side_effects=True, vmem_limit_bytes=32 * 2**20
        ),
        cost_estimate=pl.CostEstimate(
            flops=4 * 256 * 128 * 1152, bytes_accessed=1 << 20, transcendentals=0
        ),
    )(
        pltpu.with_memory_space_constraint(samples, pltpu.HBM),
        pltpu.with_memory_space_constraint(factors, pltpu.HBM),
    )


def solution(mesh):
    in_specs = (P("feat", "samp"), P("feat", None))
    out_specs = P(("feat", "samp"), None)
    return jax.shard_map(
        on_device, mesh=mesh, in_specs=in_specs, out_specs=out_specs, check_vma=False
    )
```

```python
import functools

import jax
import jax.numpy as jnp
from jax import lax
from jax.experimental import pallas as pl
from jax.experimental.pallas import tpu as pltpu
from jax.sharding import PartitionSpec as P

MESH = pl.DeviceIdType.MESH
SIDES = (("y", "x"), ("x", "y"))
CHUNKS = ((0, 0, 384, 384), (1, 512, 256, 256), (0, 384, 128, 256), (1, 768, 256, 256))
GROUPS = ((0, 1), (2, 3))
GRAM, LAST = 2, GROUPS[-1]


def contract_rows(left, right):
    return lax.dot_general(
        left, right, (((0,), (0,)), ((), ())), preferred_element_type=jnp.float32
    )


def contract_cols(left, right):
    return lax.dot_general(
        left, right, (((1,), (1,)), ((), ())), preferred_element_type=jnp.float32
    )


def kernel(sample_total, x_ref, f_ref, o_ref, fv, *refs):
    n = len(CHUNKS)
    xs, part, gotp, gotr, whole, gotz, sq = (refs[n * i:n * (i + 1)] for i in range(7))
    fs, dout, din = (refs[7 * n + 2 * i:7 * n + 2 * i + 2] for i in range(3))
    rows_out, rows_in, here, local_sem, f_send, f_recv, d_send, d_recv, send, recv, out_send, out_recv = refs[7 * n + 6:]
    feat, samp = lax.axis_index("feat"), lax.axis_index("samp")
    core = lax.rem(feat, 2)
    at = {"y": lax.rem(lax.div(feat, 2), 4), "x": lax.rem(lax.div(feat, 8), 4)}
    stride = {"y": 2, "x": 8}

    def along(axis, step, device=feat):
        there = lax.rem(at[axis] + step, 4)
        return there, (device + (there - at[axis]) * stride[axis], samp)

    other_core = feat + 1 - 2 * core
    far = (lax.rem(feat + 32, 64), samp)
    pair = (other_core, samp)

    def beside(step):
        z = lax.rem(lax.div(feat, 32) * 8 + samp + step + 16, 16)
        return (lax.rem(feat, 32) + 32 * lax.div(z, 8), lax.rem(z, 8))

    def row_owner(step):
        there = lax.rem(samp + step, 8)
        return there, (feat, there)

    barrier = pltpu.get_barrier_semaphore()
    partners = [along(axis, step, device)[1] for step in (2, 1, 3) for axis in "xy" for device in (feat, other_core)]
    partners += [pair, beside(1), beside(-1)]
    for device in partners:
        pl.semaphore_signal(barrier, inc=1, device_id=device, device_id_type=MESH)
    loads = [pltpu.make_async_copy(f_ref, fv, local_sem.at[n])]
    for c, (s, first, count, width) in enumerate(CHUNKS):
        loads.append(pltpu.make_async_copy(
            x_ref.at[:, first:first + count], xs[c].at[at[SIDES[s][0]], :, 0:count], local_sem.at[c]
        ))
    for load in loads:
        load.start()
    loads[0].wait()
    for load in loads[1:]:
        load.wait()
    pl.semaphore_wait(barrier, len(partners))

    def tell(step):
        for device in (beside(step), beside(-step)):
            pl.semaphore_signal(here.at[step // 2], inc=1, device_id=device, device_id_type=MESH)

    def hear(step):
        pl.semaphore_wait(here.at[step // 2], 2)

    tell(1)
    started = []

    def start(src, dst, send_sem, recv_sem, device):
        copy = pltpu.make_async_remote_copy(
            src_ref=src, dst_ref=dst, send_sem=send_sem, recv_sem=recv_sem,
            device_id=device, device_id_type=MESH,
        )
        copy.start()
        started.append(copy)
        return copy

    copies = {}
    for step in (2, 1, 3):
        for s, (g, r) in enumerate(SIDES):
            there, device = along(g, step)
            lanes = pl.ds(pl.multiple_of(there * 128, 128), 128)
            copies["f", s, step] = start(
                fv.at[:, lanes], fs[s].at[at[g]], f_send.at[s, step], f_recv.at[s, step], device
            )
    for group in GROUPS:
        if GRAM in group:
            column = lax.broadcasted_iota(jnp.int32, (512, 128), 1)
            chosen = samp * 64 + jnp.where(column >= 64, column - 64, column)
            pick = (lax.broadcasted_iota(jnp.int32, (512, 128), 0) == chosen).astype(jnp.bfloat16)
            own_columns = jnp.dot(fv[...], pick, preferred_element_type=jnp.float32)
            xs[GRAM][at[SIDES[0][0]], :, CHUNKS[GRAM][2]:] = own_columns.astype(jnp.bfloat16)
        for step in (2, 1, 3):
            for c in group:
                g = SIDES[CHUNKS[c][0]][0]
                there, device = along(g, step)
                copies[c, 0, step] = start(
                    xs[c].at[at[g]], xs[c].at[at[g]], send.at[c, 0, step], recv.at[c, 0, step], device
                )

    for s, (g, r) in enumerate(SIDES):
        fs[s][at[g]] = fv[:, pl.ds(pl.multiple_of(at[g] * 128, 128), 128)]
    hear(1)
    tell(2)
    weights = []
    for s in range(2):
        for step in (1, 3, 2):
            copies["f", s, step].wait_recv()
        weights.append(jnp.transpose(fs[s][...].reshape(256, 128)))

    hear(2)
    tell(4)

    def project(c):
        s, first, count, width = CHUNKS[c]
        for step in (1, 3, 2):
            copies[c, 0, step].wait_recv()
        block = jnp.dot(weights[s], xs[c][...].reshape(256, width), preferred_element_type=jnp.float32)
        part[c][...] = block.reshape(2, 4, 16, width)
        r = SIDES[s][1]
        copies[c, 1, 0] = start(part[c].at[1 - core, at[r]], gotp[c].at[0], send.at[c, 1, 0], recv.at[c, 1, 0], pair)
        for step in (2, 1, 3):
            for stage, device, there_core in ((1, other_core, 1 - core), (2, feat, core)):
                there, device = along(r, step, device)
                copies[c, stage, step] = start(
                    part[c].at[there_core, there], (gotp if stage == 1 else gotr)[c].at[step - (stage == 2)],
                    send.at[c, stage, step], recv.at[c, stage, step], device,
                )

    def exchange(c):
        r = SIDES[CHUNKS[c][0]][1]
        for step in (1, 3, 2):
            copies[c, 2, step].wait_recv()
            copies[c, 1, step].wait_recv()
        copies[c, 1, 0].wait_recv()
        same = (part[c][core, at[r]] + gotr[c][0]) + (gotr[c][1] + gotr[c][2])
        whole[c][...] = same + ((gotp[c][0] + gotp[c][1]) + (gotp[c][2] + gotp[c][3]))
        copies[c, 3] = start(whole[c], gotz[c], send.at[c, 3, 0], recv.at[c, 3, 0], far)

    def square(c):
        r, count = SIDES[CHUNKS[c][0]][1], CHUNKS[c][2]
        copies[c, 3].wait_recv()
        proj = whole[c][...] + gotz[c][...]
        squared = proj * proj
        high = squared.astype(jnp.bfloat16)
        own = sq[c].at[core, at[r]]
        if c == GRAM:
            own[:, 0:count] = high[:, 0:count]
            exact, wide = squared[:, count:], high[:, count:].astype(jnp.float32)
            lane = lax.broadcasted_iota(jnp.int32, exact.shape, 1)
            own[:, count:] = jnp.where(lane >= 64, exact - wide, wide).astype(jnp.bfloat16)
        else:
            own[...] = high
        for step in (2, 1, 3):
            for stage, core_there in ((4, feat), (5, other_core)):
                there, device = along(r, step, core_there)
                copies[c, stage, step] = start(own, own, send.at[c, stage, step], recv.at[c, stage, step], device)
        copies[c, 5, 0] = start(own, own, send.at[c, 5, 0], recv.at[c, 5, 0], pair)

    def term(c):
        s, first, count, width = CHUNKS[c]
        copies[c, 5, 0].wait_recv()
        for step in (1, 3, 2):
            copies[c, 4, step].wait_recv()
            copies[c, 5, step].wait_recv()
        left, right = xs[c][...].reshape(256, width), sq[c][...].reshape(128, width)
        product = (-6.0 / sample_total) * contract_cols(left[:, 0:count], right[:, 0:count])
        if c == GRAM:
            product = product + 6.0 * contract_cols(left[:, count:], right[:, count:])
        return product

    for k, group in enumerate(GROUPS):
        for c in group:
            project(c)
        if k == 1:
            hear(4)
        if k:
            for c in GROUPS[k - 1]:
                exchange(c)
    for c in GROUPS[-1]:
        exchange(c)
    for group in GROUPS:
        for c in group:
            square(c)
    total = [0.0, 0.0]
    for group in GROUPS:
        for c in group:
            s = CHUNKS[c][0]
            total[s] = total[s] + term(c)
            if c in LAST:
                g = SIDES[s][0]
                dout[s][...] = total[s].reshape(4, 64, 128)
                for step in (2, 1, 3):
                    there, device = along(g, step)
                    copies["d", s, step] = start(
                        dout[s].at[there], din[s].at[at[g]], d_send.at[s, step], d_recv.at[s, step], device
                    )
                din[s][at[g]] = dout[s][at[g]]
    for step in (1, 3, 2):
        for s in range(2):
            copies["d", s, step].wait_recv()
    for chunk in range(4):
        rows_out[:, chunk] = (din[0][chunk] + din[1][chunk]).reshape(8, 8, 128)
    done = []
    for order in range(7):
        there = jnp.where(samp < 4, 7 - order - jnp.where(7 - order <= samp, 1, 0), order + jnp.where(order >= samp, 1, 0))
        step = lax.rem(there + 8 - samp, 8)
        device = (feat, there)
        done.append(start(
            rows_out.at[there], rows_in.at[step - 1],
            out_send.at[step - 1], out_recv.at[step - 1], device,
        ))
    for copy in started[:-7]:
        copy.wait_send()
    for copy in done:
        copy.wait_recv()
    own = rows_out[samp]
    for slot in range(7):
        own = own + rows_in[slot]
    for chunk in range(4):
        o_ref[:, chunk * 128:(chunk + 1) * 128] = own[chunk]
    for copy in done:
        copy.wait_send()


def on_device(samples, factors):
    sample_total = samples.shape[1] * lax.axis_size("samp")
    n = len(CHUNKS)

    def each(shape, dtype):
        return [pltpu.VMEM(shape + (width,), dtype) for _, _, _, width in CHUNKS]

    scratch = [pltpu.VMEM((64, 512), jnp.bfloat16)]
    scratch += each((4, 64), jnp.bfloat16)
    scratch += each((2, 4, 16), jnp.float32)
    scratch += each((4, 16), jnp.float32)
    scratch += each((3, 16), jnp.float32)
    scratch += each((16,), jnp.float32)
    scratch += each((16,), jnp.float32)
    scratch += each((2, 4, 16), jnp.bfloat16)
    scratch += [pltpu.VMEM((4, 64, 128), jnp.bfloat16)] * 2
    scratch += [pltpu.VMEM((4, 64, 128), jnp.float32)] * 4
    scratch += [pltpu.VMEM((8, 4, 8, 128), jnp.float32), pltpu.VMEM((7, 4, 8, 128), jnp.float32)]
    scratch += [pltpu.SemaphoreType.REGULAR((3,)), pltpu.SemaphoreType.DMA((n + 1,))]
    scratch += [pltpu.SemaphoreType.DMA((2, 4))] * 4
    scratch += [pltpu.SemaphoreType.DMA((n, 6, 4)), pltpu.SemaphoreType.DMA((n, 6, 4))]
    scratch += [pltpu.SemaphoreType.DMA((7,)), pltpu.SemaphoreType.DMA((7,))]
    return pl.pallas_call(
        functools.partial(kernel, sample_total),
        out_shape=pltpu.VMEM((8, 512), jnp.float32),
        in_specs=[pl.BlockSpec(memory_space=pltpu.HBM)] * 2,
        out_specs=pl.BlockSpec(memory_space=pltpu.VMEM),
        scratch_shapes=scratch,
        compiler_params=pltpu.CompilerParams(
            collective_id=0, has_side_effects=True, vmem_limit_bytes=32 * 2**20
        ),
        cost_estimate=pl.CostEstimate(
            flops=4 * 256 * 128 * 1152, bytes_accessed=1 << 20, transcendentals=0
        ),
    )(
        pltpu.with_memory_space_constraint(samples, pltpu.HBM),
        pltpu.with_memory_space_constraint(factors, pltpu.HBM),
    )


def solution(mesh):
    in_specs = (P("feat", "samp"), P("feat", None))
    out_specs = P(("feat", "samp"), None)
    return jax.shard_map(
        on_device, mesh=mesh, in_specs=in_specs, out_specs=out_specs, check_vma=False
    )
```

```python
import functools

import jax
import jax.numpy as jnp
from jax import lax
from jax.experimental import pallas as pl
from jax.experimental.pallas import tpu as pltpu
from jax.sharding import PartitionSpec as P

MESH = pl.DeviceIdType.MESH
SIDES = (("y", "x"), ("x", "y"))
CHUNKS = ((0, 0, 384, 384), (1, 512, 256, 256), (0, 384, 128, 256), (1, 768, 256, 256))
GROUPS = ((0, 1), (2, 3))
GRAM, LAST = 2, GROUPS[-1]


def contract_rows(left, right):
    return lax.dot_general(
        left, right, (((0,), (0,)), ((), ())), preferred_element_type=jnp.float32
    )


def contract_cols(left, right):
    return lax.dot_general(
        left, right, (((1,), (1,)), ((), ())), preferred_element_type=jnp.float32
    )


def kernel(sample_total, x_ref, f_ref, o_ref, fv, *refs):
    n = len(CHUNKS)
    xs, part, got, whole, gotz, sq = (refs[n * i:n * (i + 1)] for i in range(6))
    fs, dout, din = (refs[6 * n + 2 * i:6 * n + 2 * i + 2] for i in range(3))
    rows_out, rows_in, here, local_sem, f_send, f_recv, d_send, d_recv, send, recv, out_send, out_recv = refs[6 * n + 6:]
    feat, samp = lax.axis_index("feat"), lax.axis_index("samp")
    core = lax.rem(feat, 2)
    at = {"y": lax.rem(lax.div(feat, 2), 4), "x": lax.rem(lax.div(feat, 8), 4)}
    stride = {"y": 2, "x": 8}

    def along(axis, step, device=feat):
        there = lax.rem(at[axis] + step, 4)
        return there, (device + (there - at[axis]) * stride[axis], samp)

    other_core = feat + 1 - 2 * core
    far = (lax.rem(feat + 32, 64), samp)
    pair = (other_core, samp)

    def beside(step):
        z = lax.rem(lax.div(feat, 32) * 8 + samp + step + 16, 16)
        return (lax.rem(feat, 32) + 32 * lax.div(z, 8), lax.rem(z, 8))

    def row_owner(step):
        there = lax.rem(samp + step, 8)
        return there, (feat, there)

    barrier = pltpu.get_barrier_semaphore()
    partners = [along(axis, step, device)[1] for step in (2, 1, 3) for axis in "xy" for device in (feat, other_core)]
    partners += [pair, beside(1), beside(-1)]
    for device in partners:
        pl.semaphore_signal(barrier, inc=1, device_id=device, device_id_type=MESH)
    loads = [pltpu.make_async_copy(f_ref, fv, local_sem.at[n])]
    for c, (s, first, count, width) in enumerate(CHUNKS):
        loads.append(pltpu.make_async_copy(
            x_ref.at[:, first:first + count], xs[c].at[at[SIDES[s][0]], :, 0:count], local_sem.at[c]
        ))
    for load in loads:
        load.start()
    loads[0].wait()
    for load in loads[1:]:
        load.wait()
    pl.semaphore_wait(barrier, len(partners))

    def tell(step):
        for device in (beside(step), beside(-step)):
            pl.semaphore_signal(here.at[step // 2], inc=1, device_id=device, device_id_type=MESH)

    def hear(step):
        pl.semaphore_wait(here.at[step // 2], 2)

    tell(1)
    def start(src, dst, send_sem, recv_sem, device):
        pltpu.make_async_remote_copy(
            src_ref=src, dst_ref=dst, send_sem=send_sem, recv_sem=recv_sem,
            device_id=device, device_id_type=MESH,
        ).start()

    def wait(ref, sem):
        pltpu.make_async_copy(ref, ref, sem).wait()

    for step in (2, 1, 3):
        for s, (g, r) in enumerate(SIDES):
            there, device = along(g, step)
            lanes = pl.ds(pl.multiple_of(there * 128, 128), 128)
            start(
                fv.at[:, lanes], fs[s].at[at[g]], f_send.at[s], f_recv.at[s], device
            )
    for group in GROUPS:
        if GRAM in group:
            column = lax.broadcasted_iota(jnp.int32, (512, 128), 1)
            chosen = samp * 64 + jnp.where(column >= 64, column - 64, column)
            pick = (lax.broadcasted_iota(jnp.int32, (512, 128), 0) == chosen).astype(jnp.bfloat16)
            own_columns = jnp.dot(fv[...], pick, preferred_element_type=jnp.float32)
            xs[GRAM][at[SIDES[0][0]], :, CHUNKS[GRAM][2]:] = own_columns.astype(jnp.bfloat16)
        for step in (2, 1, 3):
            for c in group:
                g = SIDES[CHUNKS[c][0]][0]
                there, device = along(g, step)
                start(
                    xs[c].at[at[g]], xs[c].at[at[g]], send.at[c, 0], recv.at[c, 0], device
                )

    for s, (g, r) in enumerate(SIDES):
        fs[s][at[g]] = fv[:, pl.ds(pl.multiple_of(at[g] * 128, 128), 128)]
    hear(1)
    tell(2)
    weights = []
    for s in range(2):
        wait(fs[s].at[0:3], f_recv.at[s])
        weights.append(jnp.transpose(fs[s][...].reshape(256, 128)))

    hear(2)
    tell(4)

    def project(c):
        s, first, count, width = CHUNKS[c]
        wait(xs[c].at[0:3], recv.at[c, 0])
        block = jnp.dot(weights[s], xs[c][...].reshape(256, width), preferred_element_type=jnp.float32)
        part[c][...] = block.reshape(2, 4, 16, width)
        r = SIDES[s][1]
        start(part[c].at[1 - core, at[r]], got[c].at[0], send.at[c, 1], recv.at[c, 1], pair)
        for step in (2, 1, 3):
            for slot, device, there_core in ((step, other_core, 1 - core), (3 + step, feat, core)):
                there, device = along(r, step, device)
                start(
                    part[c].at[there_core, there], got[c].at[slot], send.at[c, 1], recv.at[c, 1], device
                )

    def exchange(c):
        r = SIDES[CHUNKS[c][0]][1]
        wait(got[c], recv.at[c, 1])
        whole[c][...] = ((part[c][core, at[r]] + got[c][0]) + (got[c][1] + got[c][2])) + (
            (got[c][3] + got[c][4]) + (got[c][5] + got[c][6])
        )
        start(whole[c], gotz[c], send.at[c, 2], recv.at[c, 2], far)

    def square(c):
        r, count = SIDES[CHUNKS[c][0]][1], CHUNKS[c][2]
        wait(gotz[c], recv.at[c, 2])
        proj = whole[c][...] + gotz[c][...]
        squared = proj * proj
        high = squared.astype(jnp.bfloat16)
        own = sq[c].at[core * 4 + at[r]]
        if c == GRAM:
            own[:, 0:count] = high[:, 0:count]
            exact, wide = squared[:, count:], high[:, count:].astype(jnp.float32)
            lane = lax.broadcasted_iota(jnp.int32, exact.shape, 1)
            own[:, count:] = jnp.where(lane >= 64, exact - wide, wide).astype(jnp.bfloat16)
        else:
            own[...] = high
        for step in (2, 1, 3):
            for core_there in (feat, other_core):
                there, device = along(r, step, core_there)
                start(own, own, send.at[c, 3], recv.at[c, 3], device)
        start(own, own, send.at[c, 3], recv.at[c, 3], pair)

    def term(c):
        s, first, count, width = CHUNKS[c]
        wait(sq[c].at[0:7], recv.at[c, 3])
        left, right = xs[c][...].reshape(256, width), sq[c][...].reshape(128, width)
        product = (-6.0 / sample_total) * contract_cols(left[:, 0:count], right[:, 0:count])
        if c == GRAM:
            product = product + 6.0 * contract_cols(left[:, count:], right[:, count:])
        return product

    for k, group in enumerate(GROUPS):
        for c in group:
            project(c)
        if k == 1:
            hear(4)
        if k:
            for c in GROUPS[k - 1]:
                exchange(c)
    for c in GROUPS[-1]:
        exchange(c)
    for group in GROUPS:
        for c in group:
            square(c)
    total = [0.0, 0.0]
    for group in GROUPS:
        for c in group:
            s = CHUNKS[c][0]
            total[s] = total[s] + term(c)
            if c in LAST:
                g = SIDES[s][0]
                dout[s][...] = total[s].reshape(4, 64, 128)
                for step in (2, 1, 3):
                    there, device = along(g, step)
                    start(
                        dout[s].at[there], din[s].at[at[g]], d_send.at[s], d_recv.at[s], device
                    )
                din[s][at[g]] = dout[s][at[g]]
    for s in range(2):
        wait(din[s].at[0:3], d_recv.at[s])
    for chunk in range(4):
        rows_out[:, chunk] = (din[0][chunk] + din[1][chunk]).reshape(8, 8, 128)
    for order in range(7):
        there = jnp.where(samp < 4, 7 - order - jnp.where(7 - order <= samp, 1, 0), order + jnp.where(order >= samp, 1, 0))
        step = lax.rem(there + 8 - samp, 8)
        device = (feat, there)
        start(rows_out.at[there], rows_in.at[step - 1], out_send, out_recv, device)
    for s in range(2):
        wait(fs[s].at[0:3], f_send.at[s])
        wait(dout[s].at[0:3], d_send.at[s])
    for c in range(n):
        wait(xs[c].at[0:3], send.at[c, 0])
        wait(got[c], send.at[c, 1])
        wait(whole[c], send.at[c, 2])
        wait(sq[c].at[0:7], send.at[c, 3])
    wait(rows_in, out_recv)
    own = rows_out[samp]
    for slot in range(7):
        own = own + rows_in[slot]
    for chunk in range(4):
        o_ref[:, chunk * 128:(chunk + 1) * 128] = own[chunk]
    wait(rows_in, out_send)


def on_device(samples, factors):
    sample_total = samples.shape[1] * lax.axis_size("samp")
    n = len(CHUNKS)

    def each(shape, dtype):
        return [pltpu.VMEM(shape + (width,), dtype) for _, _, _, width in CHUNKS]

    scratch = [pltpu.VMEM((64, 512), jnp.bfloat16)]
    scratch += each((4, 64), jnp.bfloat16)
    scratch += each((2, 4, 16), jnp.float32)
    scratch += each((7, 16), jnp.float32)
    scratch += each((16,), jnp.float32)
    scratch += each((16,), jnp.float32)
    scratch += each((8, 16), jnp.bfloat16)
    scratch += [pltpu.VMEM((4, 64, 128), jnp.bfloat16)] * 2
    scratch += [pltpu.VMEM((4, 64, 128), jnp.float32)] * 4
    scratch += [pltpu.VMEM((8, 4, 8, 128), jnp.float32), pltpu.VMEM((7, 4, 8, 128), jnp.float32)]
    scratch += [pltpu.SemaphoreType.REGULAR((3,)), pltpu.SemaphoreType.DMA((n + 1,))]
    scratch += [pltpu.SemaphoreType.DMA((2,))] * 4
    scratch += [pltpu.SemaphoreType.DMA((n, 4))] * 2
    scratch += [pltpu.SemaphoreType.DMA] * 2
    return pl.pallas_call(
        functools.partial(kernel, sample_total),
        out_shape=pltpu.VMEM((8, 512), jnp.float32),
        in_specs=[pl.BlockSpec(memory_space=pltpu.HBM)] * 2,
        out_specs=pl.BlockSpec(memory_space=pltpu.VMEM),
        scratch_shapes=scratch,
        compiler_params=pltpu.CompilerParams(
            collective_id=0, has_side_effects=True, vmem_limit_bytes=32 * 2**20
        ),
        cost_estimate=pl.CostEstimate(
            flops=4 * 256 * 128 * 1152, bytes_accessed=1 << 20, transcendentals=0
        ),
    )(
        pltpu.with_memory_space_constraint(samples, pltpu.HBM),
        pltpu.with_memory_space_constraint(factors, pltpu.HBM),
    )


def solution(mesh):
    in_specs = (P("feat", "samp"), P("feat", None))
    out_specs = P(("feat", "samp"), None)
    return jax.shard_map(
        on_device, mesh=mesh, in_specs=in_specs, out_specs=out_specs, check_vma=False
    )
```

```python
import functools

import jax
import jax.numpy as jnp
from jax import lax
from jax.experimental import pallas as pl
from jax.experimental.pallas import tpu as pltpu
from jax.sharding import PartitionSpec as P

MESH = pl.DeviceIdType.MESH
SIDES = (("y", "x"), ("x", "y"))
CHUNKS = ((0, 0, 384, 384), (1, 512, 256, 256), (0, 384, 128, 256), (1, 768, 256, 256))
GROUPS = ((0, 1), (2, 3))
GRAM, LAST = 2, GROUPS[-1]


def contract_rows(left, right):
    return lax.dot_general(
        left, right, (((0,), (0,)), ((), ())), preferred_element_type=jnp.float32
    )


def contract_cols(left, right):
    return lax.dot_general(
        left, right, (((1,), (1,)), ((), ())), preferred_element_type=jnp.float32
    )


def kernel(sample_total, x_ref, f_ref, o_ref, fv, *refs):
    n = len(CHUNKS)
    xs, part, got, whole, gotz, sq = (refs[n * i:n * (i + 1)] for i in range(6))
    fs, dout, din = (refs[6 * n + 2 * i:6 * n + 2 * i + 2] for i in range(3))
    rows_out, rows_in, here, local_sem, f_send, f_recv, d_send, d_recv, send, recv, out_send, out_recv = refs[6 * n + 6:]
    feat, samp = lax.axis_index("feat"), lax.axis_index("samp")
    core = lax.rem(feat, 2)
    at = {"y": lax.rem(lax.div(feat, 2), 4), "x": lax.rem(lax.div(feat, 8), 4)}
    stride = {"y": 2, "x": 8}

    def along(axis, step, device=feat):
        there = lax.rem(at[axis] + step, 4)
        return there, (device + (there - at[axis]) * stride[axis], samp)

    other_core = feat + 1 - 2 * core
    far = (lax.rem(feat + 32, 64), samp)
    pair = (other_core, samp)

    def beside(step):
        z = lax.rem(lax.div(feat, 32) * 8 + samp + step + 16, 16)
        return (lax.rem(feat, 32) + 32 * lax.div(z, 8), lax.rem(z, 8))

    def row_owner(step):
        there = lax.rem(samp + step, 8)
        return there, (feat, there)

    barrier = pltpu.get_barrier_semaphore()
    partners = [along(axis, step, device)[1] for step in (2, 1, 3) for axis in "xy" for device in (feat, other_core)]
    partners += [pair, beside(1), beside(-1)]
    for device in partners:
        pl.semaphore_signal(barrier, inc=1, device_id=device, device_id_type=MESH)
    loads = [pltpu.make_async_copy(f_ref, fv, local_sem.at[n])]
    for c, (s, first, count, width) in enumerate(CHUNKS):
        loads.append(pltpu.make_async_copy(
            x_ref.at[:, first:first + count], xs[c].at[at[SIDES[s][0]], :, 0:count], local_sem.at[c]
        ))
    for load in loads:
        load.start()
    loads[0].wait()
    column = lax.broadcasted_iota(jnp.int32, (512, 128), 1)
    chosen = samp * 64 + jnp.where(column >= 64, column - 64, column)
    pick = (lax.broadcasted_iota(jnp.int32, (512, 128), 0) == chosen).astype(jnp.bfloat16)
    own_columns = jnp.dot(fv[...], pick, preferred_element_type=jnp.float32)
    xs[GRAM][at[SIDES[0][0]], :, CHUNKS[GRAM][2]:] = own_columns.astype(jnp.bfloat16)
    for load in loads[1:]:
        load.wait()
    pl.semaphore_wait(barrier, len(partners))

    def tell(step):
        for device in (beside(step), beside(-step)):
            pl.semaphore_signal(here.at[step // 2], inc=1, device_id=device, device_id_type=MESH)

    def hear(step):
        pl.semaphore_wait(here.at[step // 2], 2)

    tell(1)
    def start(src, dst, send_sem, recv_sem, device):
        pltpu.make_async_remote_copy(
            src_ref=src, dst_ref=dst, send_sem=send_sem, recv_sem=recv_sem,
            device_id=device, device_id_type=MESH,
        ).start()

    def wait(ref, sem):
        pltpu.make_async_copy(ref, ref, sem).wait()

    for step in (2, 1, 3):
        for s, (g, r) in enumerate(SIDES):
            there, device = along(g, step)
            lanes = pl.ds(pl.multiple_of(there * 128, 128), 128)
            start(
                fv.at[:, lanes], fs[s].at[at[g]], f_send.at[s], f_recv.at[s], device
            )
    for group in GROUPS:
        for step in (2, 1, 3):
            for c in group:
                g = SIDES[CHUNKS[c][0]][0]
                there, device = along(g, step)
                start(
                    xs[c].at[at[g]], xs[c].at[at[g]], send.at[c, 0], recv.at[c, 0], device
                )

    for s, (g, r) in enumerate(SIDES):
        fs[s][at[g]] = fv[:, pl.ds(pl.multiple_of(at[g] * 128, 128), 128)]
    hear(1)
    tell(2)
    weights = []
    for s in range(2):
        wait(fs[s].at[0:3], f_recv.at[s])
        weights.append(jnp.transpose(fs[s][...].reshape(256, 128)))

    hear(2)
    tell(4)

    def project(c):
        s, first, count, width = CHUNKS[c]
        wait(xs[c].at[0:3], recv.at[c, 0])
        block = jnp.dot(weights[s], xs[c][...].reshape(256, width), preferred_element_type=jnp.float32)
        part[c][...] = block.reshape(2, 4, 16, width)
        r = SIDES[s][1]
        start(part[c].at[1 - core, at[r]], got[c].at[0], send.at[c, 1], recv.at[c, 1], pair)
        for step in (2, 1, 3):
            for slot, device, there_core in ((step, other_core, 1 - core), (3 + step, feat, core)):
                there, device = along(r, step, device)
                start(
                    part[c].at[there_core, there], got[c].at[slot], send.at[c, 1], recv.at[c, 1], device
                )

    def exchange(c):
        r = SIDES[CHUNKS[c][0]][1]
        wait(got[c], recv.at[c, 1])
        whole[c][...] = ((part[c][core, at[r]] + got[c][0]) + (got[c][1] + got[c][2])) + (
            (got[c][3] + got[c][4]) + (got[c][5] + got[c][6])
        )
        start(whole[c], gotz[c], send.at[c, 2], recv.at[c, 2], far)

    def square(c):
        r, count = SIDES[CHUNKS[c][0]][1], CHUNKS[c][2]
        wait(gotz[c], recv.at[c, 2])
        proj = whole[c][...] + gotz[c][...]
        squared = proj * proj
        high = squared.astype(jnp.bfloat16)
        own = sq[c].at[core * 4 + at[r]]
        if c == GRAM:
            own[:, 0:count] = high[:, 0:count]
            exact, wide = squared[:, count:], high[:, count:].astype(jnp.float32)
            lane = lax.broadcasted_iota(jnp.int32, exact.shape, 1)
            own[:, count:] = jnp.where(lane >= 64, exact - wide, wide).astype(jnp.bfloat16)
        else:
            own[...] = high
        for step in (2, 1, 3):
            for core_there in (feat, other_core):
                there, device = along(r, step, core_there)
                start(own, own, send.at[c, 3], recv.at[c, 3], device)
        start(own, own, send.at[c, 3], recv.at[c, 3], pair)

    def term(c):
        s, first, count, width = CHUNKS[c]
        wait(sq[c].at[0:7], recv.at[c, 3])
        left, right = xs[c][...].reshape(256, width), sq[c][...].reshape(128, width)
        product = (-6.0 / sample_total) * contract_cols(left[:, 0:count], right[:, 0:count])
        if c == GRAM:
            product = product + 6.0 * contract_cols(left[:, count:], right[:, count:])
        return product

    for k, group in enumerate(GROUPS):
        for c in group:
            project(c)
        if k == 1:
            hear(4)
        if k:
            for c in GROUPS[k - 1]:
                exchange(c)
    for c in GROUPS[-1]:
        exchange(c)
    for group in GROUPS:
        for c in group:
            square(c)
    total = [0.0, 0.0]
    for group in GROUPS:
        for c in group:
            s = CHUNKS[c][0]
            total[s] = total[s] + term(c)
            if c in LAST:
                g = SIDES[s][0]
                dout[s][...] = total[s].reshape(4, 64, 128)
                for step in (2, 1, 3):
                    there, device = along(g, step)
                    start(
                        dout[s].at[there], din[s].at[at[g]], d_send.at[s], d_recv.at[s], device
                    )
                din[s][at[g]] = dout[s][at[g]]
    for s in range(2):
        wait(din[s].at[0:3], d_recv.at[s])
    for chunk in range(4):
        rows_out[:, chunk] = (din[0][chunk] + din[1][chunk]).reshape(8, 8, 128)
    for order in range(7):
        there = jnp.where(samp < 4, 7 - order - jnp.where(7 - order <= samp, 1, 0), order + jnp.where(order >= samp, 1, 0))
        step = lax.rem(there + 8 - samp, 8)
        device = (feat, there)
        start(rows_out.at[there], rows_in.at[step - 1], out_send, out_recv, device)
    for s in range(2):
        wait(fs[s].at[0:3], f_send.at[s])
        wait(dout[s].at[0:3], d_send.at[s])
    for c in range(n):
        wait(xs[c].at[0:3], send.at[c, 0])
        wait(got[c], send.at[c, 1])
        wait(whole[c], send.at[c, 2])
        wait(sq[c].at[0:7], send.at[c, 3])
    wait(rows_in, out_recv)
    own = rows_out[samp]
    for slot in range(7):
        own = own + rows_in[slot]
    for chunk in range(4):
        o_ref[:, chunk * 128:(chunk + 1) * 128] = own[chunk]
    wait(rows_in, out_send)


def on_device(samples, factors):
    sample_total = samples.shape[1] * lax.axis_size("samp")
    n = len(CHUNKS)

    def each(shape, dtype):
        return [pltpu.VMEM(shape + (width,), dtype) for _, _, _, width in CHUNKS]

    scratch = [pltpu.VMEM((64, 512), jnp.bfloat16)]
    scratch += each((4, 64), jnp.bfloat16)
    scratch += each((2, 4, 16), jnp.float32)
    scratch += each((7, 16), jnp.float32)
    scratch += each((16,), jnp.float32)
    scratch += each((16,), jnp.float32)
    scratch += each((8, 16), jnp.bfloat16)
    scratch += [pltpu.VMEM((4, 64, 128), jnp.bfloat16)] * 2
    scratch += [pltpu.VMEM((4, 64, 128), jnp.float32)] * 4
    scratch += [pltpu.VMEM((8, 4, 8, 128), jnp.float32), pltpu.VMEM((7, 4, 8, 128), jnp.float32)]
    scratch += [pltpu.SemaphoreType.REGULAR((3,)), pltpu.SemaphoreType.DMA((n + 1,))]
    scratch += [pltpu.SemaphoreType.DMA((2,))] * 4
    scratch += [pltpu.SemaphoreType.DMA((n, 4))] * 2
    scratch += [pltpu.SemaphoreType.DMA] * 2
    return pl.pallas_call(
        functools.partial(kernel, sample_total),
        out_shape=pltpu.VMEM((8, 512), jnp.float32),
        in_specs=[pl.BlockSpec(memory_space=pltpu.HBM)] * 2,
        out_specs=pl.BlockSpec(memory_space=pltpu.VMEM),
        scratch_shapes=scratch,
        compiler_params=pltpu.CompilerParams(
            collective_id=0, has_side_effects=True, vmem_limit_bytes=32 * 2**20
        ),
        cost_estimate=pl.CostEstimate(
            flops=4 * 256 * 128 * 1152, bytes_accessed=1 << 20, transcendentals=0
        ),
    )(
        pltpu.with_memory_space_constraint(samples, pltpu.HBM),
        pltpu.with_memory_space_constraint(factors, pltpu.HBM),
    )


def solution(mesh):
    in_specs = (P("feat", "samp"), P("feat", None))
    out_specs = P(("feat", "samp"), None)
    return jax.shard_map(
        on_device, mesh=mesh, in_specs=in_specs, out_specs=out_specs, check_vma=False
    )
```

```python
import functools

import jax
import jax.numpy as jnp
from jax import lax
from jax.experimental import pallas as pl
from jax.experimental.pallas import tpu as pltpu
from jax.sharding import PartitionSpec as P

MESH = pl.DeviceIdType.MESH
SIDES = (("y", "x"), ("x", "y"))
CHUNKS = ((0, 0, 384, 384), (1, 512, 256, 256), (0, 384, 128, 256), (1, 768, 256, 256))
GROUPS = ((0, 1), (2, 3))
GRAM, LAST = 2, GROUPS[-1]


def contract_rows(left, right):
    return lax.dot_general(
        left, right, (((0,), (0,)), ((), ())), preferred_element_type=jnp.float32
    )


def contract_cols(left, right):
    return lax.dot_general(
        left, right, (((1,), (1,)), ((), ())), preferred_element_type=jnp.float32
    )


def kernel(sample_total, x_ref, f_ref, o_ref, fv, *refs):
    n = len(CHUNKS)
    xs, part, got, whole, gotz, sq = (refs[n * i:n * (i + 1)] for i in range(6))
    fs, dout, din = (refs[6 * n + 2 * i:6 * n + 2 * i + 2] for i in range(3))
    rows_out, rows_in, here, local_sem, f_send, f_recv, d_send, d_recv, send, recv, out_send, out_recv = refs[6 * n + 6:]
    feat, samp = lax.axis_index("feat"), lax.axis_index("samp")
    core = lax.rem(feat, 2)
    at = {"y": lax.rem(lax.div(feat, 2), 4), "x": lax.rem(lax.div(feat, 8), 4)}
    stride = {"y": 2, "x": 8}

    def along(axis, step, device=feat):
        there = lax.rem(at[axis] + step, 4)
        return there, (device + (there - at[axis]) * stride[axis], samp)

    other_core = feat + 1 - 2 * core
    far = (lax.rem(feat + 32, 64), samp)
    pair = (other_core, samp)

    def beside(step):
        z = lax.rem(lax.div(feat, 32) * 8 + samp + step + 16, 16)
        return (lax.rem(feat, 32) + 32 * lax.div(z, 8), lax.rem(z, 8))

    def row_owner(step):
        there = lax.rem(samp + step, 8)
        return there, (feat, there)

    barrier = pltpu.get_barrier_semaphore()
    partners = [along(axis, step, device)[1] for step in (2, 1, 3) for axis in "xy" for device in (feat, other_core)]
    partners += [pair, beside(1), beside(-1), beside(2), beside(-2)]
    for device in partners:
        pl.semaphore_signal(barrier, inc=1, device_id=device, device_id_type=MESH)
    loads = [pltpu.make_async_copy(f_ref, fv, local_sem.at[n])]
    for c, (s, first, count, width) in enumerate(CHUNKS):
        loads.append(pltpu.make_async_copy(
            x_ref.at[:, first:first + count], xs[c].at[at[SIDES[s][0]], :, 0:count], local_sem.at[c]
        ))
    for load in loads:
        load.start()
    loads[0].wait()
    column = lax.broadcasted_iota(jnp.int32, (512, 128), 1)
    chosen = samp * 64 + jnp.where(column >= 64, column - 64, column)
    pick = (lax.broadcasted_iota(jnp.int32, (512, 128), 0) == chosen).astype(jnp.bfloat16)
    own_columns = jnp.dot(fv[...], pick, preferred_element_type=jnp.float32)
    xs[GRAM][at[SIDES[0][0]], :, CHUNKS[GRAM][2]:] = own_columns.astype(jnp.bfloat16)
    for load in loads[1:]:
        load.wait()
    pl.semaphore_wait(barrier, len(partners))

    def tell(step):
        for device in (beside(step), beside(-step)):
            pl.semaphore_signal(here.at[step // 4], inc=1, device_id=device, device_id_type=MESH)

    def hear(step):
        pl.semaphore_wait(here.at[step // 4], 2)

    tell(2)
    def start(src, dst, send_sem, recv_sem, device):
        pltpu.make_async_remote_copy(
            src_ref=src, dst_ref=dst, send_sem=send_sem, recv_sem=recv_sem,
            device_id=device, device_id_type=MESH,
        ).start()

    def wait(ref, sem):
        pltpu.make_async_copy(ref, ref, sem).wait()

    for step in (2, 1, 3):
        for s, (g, r) in enumerate(SIDES):
            there, device = along(g, step)
            lanes = pl.ds(pl.multiple_of(there * 128, 128), 128)
            start(
                fv.at[:, lanes], fs[s].at[at[g]], f_send.at[s], f_recv.at[s], device
            )
    for group in GROUPS:
        for step in (2, 1, 3):
            for c in group:
                g = SIDES[CHUNKS[c][0]][0]
                there, device = along(g, step)
                start(
                    xs[c].at[at[g]], xs[c].at[at[g]], send.at[c, 0], recv.at[c, 0], device
                )

    for s, (g, r) in enumerate(SIDES):
        fs[s][at[g]] = fv[:, pl.ds(pl.multiple_of(at[g] * 128, 128), 128)]
    weights = []
    for s in range(2):
        wait(fs[s].at[0:3], f_recv.at[s])
        weights.append(jnp.transpose(fs[s][...].reshape(256, 128)))

    hear(2)
    tell(4)

    def project(c):
        s, first, count, width = CHUNKS[c]
        wait(xs[c].at[0:3], recv.at[c, 0])
        block = jnp.dot(weights[s], xs[c][...].reshape(256, width), preferred_element_type=jnp.float32)
        part[c][...] = block.reshape(2, 4, 16, width)
        r = SIDES[s][1]
        start(part[c].at[1 - core, at[r]], got[c].at[0], send.at[c, 1], recv.at[c, 1], pair)
        for step in (2, 1, 3):
            for slot, device, there_core in ((step, other_core, 1 - core), (3 + step, feat, core)):
                there, device = along(r, step, device)
                start(
                    part[c].at[there_core, there], got[c].at[slot], send.at[c, 1], recv.at[c, 1], device
                )

    def exchange(c):
        r = SIDES[CHUNKS[c][0]][1]
        wait(got[c], recv.at[c, 1])
        whole[c][...] = ((part[c][core, at[r]] + got[c][0]) + (got[c][1] + got[c][2])) + (
            (got[c][3] + got[c][4]) + (got[c][5] + got[c][6])
        )
        start(whole[c], gotz[c], send.at[c, 2], recv.at[c, 2], far)

    def square(c):
        r, count = SIDES[CHUNKS[c][0]][1], CHUNKS[c][2]
        wait(gotz[c], recv.at[c, 2])
        proj = whole[c][...] + gotz[c][...]
        squared = proj * proj
        high = squared.astype(jnp.bfloat16)
        own = sq[c].at[core * 4 + at[r]]
        if c == GRAM:
            own[:, 0:count] = high[:, 0:count]
            exact, wide = squared[:, count:], high[:, count:].astype(jnp.float32)
            lane = lax.broadcasted_iota(jnp.int32, exact.shape, 1)
            own[:, count:] = jnp.where(lane >= 64, exact - wide, wide).astype(jnp.bfloat16)
        else:
            own[...] = high
        for step in (2, 1, 3):
            for core_there in (feat, other_core):
                there, device = along(r, step, core_there)
                start(own, own, send.at[c, 3], recv.at[c, 3], device)
        start(own, own, send.at[c, 3], recv.at[c, 3], pair)

    def term(c):
        s, first, count, width = CHUNKS[c]
        wait(sq[c].at[0:7], recv.at[c, 3])
        left, right = xs[c][...].reshape(256, width), sq[c][...].reshape(128, width)
        product = (-6.0 / sample_total) * contract_cols(left[:, 0:count], right[:, 0:count])
        if c == GRAM:
            product = product + 6.0 * contract_cols(left[:, count:], right[:, count:])
        return product

    for k, group in enumerate(GROUPS):
        for c in group:
            project(c)
        if k == 1:
            hear(4)
        if k:
            for c in GROUPS[k - 1]:
                exchange(c)
    for c in GROUPS[-1]:
        exchange(c)
    for group in GROUPS:
        for c in group:
            square(c)
    total = [0.0, 0.0]
    for group in GROUPS:
        for c in group:
            s = CHUNKS[c][0]
            total[s] = total[s] + term(c)
            if c in LAST:
                g = SIDES[s][0]
                dout[s][...] = total[s].reshape(4, 64, 128)
                for step in (2, 1, 3):
                    there, device = along(g, step)
                    start(
                        dout[s].at[there], din[s].at[at[g]], d_send.at[s], d_recv.at[s], device
                    )
                din[s][at[g]] = dout[s][at[g]]
    for s in range(2):
        wait(din[s].at[0:3], d_recv.at[s])
    for chunk in range(4):
        rows_out[:, chunk] = (din[0][chunk] + din[1][chunk]).reshape(8, 8, 128)
    for order in range(7):
        there = jnp.where(samp < 4, 7 - order - jnp.where(7 - order <= samp, 1, 0), order + jnp.where(order >= samp, 1, 0))
        step = lax.rem(there + 8 - samp, 8)
        device = (feat, there)
        start(rows_out.at[there], rows_in.at[step - 1], out_send, out_recv, device)
    for s in range(2):
        wait(fs[s].at[0:3], f_send.at[s])
        wait(dout[s].at[0:3], d_send.at[s])
    for c in range(n):
        wait(xs[c].at[0:3], send.at[c, 0])
        wait(got[c], send.at[c, 1])
        wait(whole[c], send.at[c, 2])
        wait(sq[c].at[0:7], send.at[c, 3])
    wait(rows_in, out_recv)
    own = rows_out[samp]
    for slot in range(7):
        own = own + rows_in[slot]
    for chunk in range(4):
        o_ref[:, chunk * 128:(chunk + 1) * 128] = own[chunk]
    wait(rows_in, out_send)


def on_device(samples, factors):
    sample_total = samples.shape[1] * lax.axis_size("samp")
    n = len(CHUNKS)

    def each(shape, dtype):
        return [pltpu.VMEM(shape + (width,), dtype) for _, _, _, width in CHUNKS]

    scratch = [pltpu.VMEM((64, 512), jnp.bfloat16)]
    scratch += each((4, 64), jnp.bfloat16)
    scratch += each((2, 4, 16), jnp.float32)
    scratch += each((7, 16), jnp.float32)
    scratch += each((16,), jnp.float32)
    scratch += each((16,), jnp.float32)
    scratch += each((8, 16), jnp.bfloat16)
    scratch += [pltpu.VMEM((4, 64, 128), jnp.bfloat16)] * 2
    scratch += [pltpu.VMEM((4, 64, 128), jnp.float32)] * 4
    scratch += [pltpu.VMEM((8, 4, 8, 128), jnp.float32), pltpu.VMEM((7, 4, 8, 128), jnp.float32)]
    scratch += [pltpu.SemaphoreType.REGULAR((2,)), pltpu.SemaphoreType.DMA((n + 1,))]
    scratch += [pltpu.SemaphoreType.DMA((2,))] * 4
    scratch += [pltpu.SemaphoreType.DMA((n, 4))] * 2
    scratch += [pltpu.SemaphoreType.DMA] * 2
    return pl.pallas_call(
        functools.partial(kernel, sample_total),
        out_shape=pltpu.VMEM((8, 512), jnp.float32),
        in_specs=[pl.BlockSpec(memory_space=pltpu.HBM)] * 2,
        out_specs=pl.BlockSpec(memory_space=pltpu.VMEM),
        scratch_shapes=scratch,
        compiler_params=pltpu.CompilerParams(
            collective_id=0, has_side_effects=True, vmem_limit_bytes=32 * 2**20
        ),
        cost_estimate=pl.CostEstimate(
            flops=4 * 256 * 128 * 1152, bytes_accessed=1 << 20, transcendentals=0
        ),
    )(
        pltpu.with_memory_space_constraint(samples, pltpu.HBM),
        pltpu.with_memory_space_constraint(factors, pltpu.HBM),
    )


def solution(mesh):
    in_specs = (P("feat", "samp"), P("feat", None))
    out_specs = P(("feat", "samp"), None)
    return jax.shard_map(
        on_device, mesh=mesh, in_specs=in_specs, out_specs=out_specs, check_vma=False
    )
```
